32 devices in a mesh: section: 2 (over x), dp: 8 (over z, y), context: 2 (over core).
Axes of the slice: x: 2, y: 2, z: 4, core: 2. Of those that a mesh axis runs over, the one named last changes fastest.
Arguments:
- hidden_in: bfloat16 [32, 1024, 384], P('dp', 'context'), may hold values from -6 to 6
- cotangent: bfloat16 [32, 1024, 384], P('dp', 'context'), may hold values from -6 to 6
- ada_w: bfloat16 [2, 384, 2304], P('section', 'dp'), may hold values from -0.3125 to 0.3125
- ada_b: bfloat16 [2, 2304], P('section', 'dp'), may hold values from -1.5 to 1.5
- qkv_w: bfloat16 [2, 384, 1152], P('section', 'dp'), may hold values from -0.3125 to 0.3125
- proj_w: bfloat16 [2, 384, 384], P('section', 'dp'), may hold values from -0.625 to 0.625
- mlp_in_w: bfloat16 [2, 384, 1536], P('section', 'dp'), may hold values from -0.3125 to 0.3125
- mlp_out_w: bfloat16 [2, 1536, 384], P('section', 'dp'), may hold values from -0.15625 to 0.15625
- class_table: bfloat16 [1001, 384], P(None, 'dp'), may hold values from -6 to 6
- timesteps: int32 [32], P('dp'), may hold values from 0 to 999
- labels: int32 [32], P('dp'), may hold values from 0 to 1000
Outputs:
- hidden_states: bfloat16 [2, 32, 1024, 384], P('section', 'dp', 'context')
- input_grads: bfloat16 [2, 32, 1024, 384], P('section', 'dp', 'context')
- grad_ada_w: float32 [2, 384, 2304], P('section', 'dp')
- grad_ada_b: float32 [2, 2304], P('section', 'dp')
- grad_qkv_w: float32 [2, 384, 1152], P('section', 'dp')
- grad_proj_w: float32 [2, 384, 384], P('section', 'dp')
- grad_mlp_in_w: float32 [2, 384, 1536], P('section', 'dp')
- grad_mlp_out_w: float32 [2, 1536, 384], P('section', 'dp')
- grad_class_table: float32 [1001, 384], P(None, 'dp')
The draws below stay inside these ranges and needn't reach their ends.
All inputs are finite; a program needn't handle non-finite values.
Results may differ from the reference program's by a relative error of at most 0.017.
Values may be sent and summed in bfloat16 or wider, within the bound.
A program may use at most 448 MiB of HBM per device.

```python
import math
import jax
import jax.numpy as jnp
from jax import lax

D = 384
HEADS = 6
HDIM = 64
FF = 1536
SEQ = 1024
NCLASS = 1001
NSTEPS = 1000
LATENTS = 32


def touch_ends(result, stream_key, low, high):
    place = [jax.random.randint(jax.random.fold_in(stream_key, axis), (), 0, length) for axis, length in enumerate(result.shape)]
    widest = result.shape.index(max(result.shape))
    beside = place[:widest] + [(place[widest] + 1) % result.shape[widest]] + place[widest + 1:]
    return result.at[tuple(place)].set(low).at[tuple(beside)].set(high)


def steps_of(stream_key, dims, cuts, least, high):
    loudness, own = 1.0, jax.random.fold_in(stream_key, 6)
    for axis_at, parts in cuts:
        heights = jnp.exp(jax.random.uniform(jax.random.fold_in(own, axis_at), (parts,), jnp.float32, least / len(cuts), high / len(cuts)))
        loudness = loudness * jnp.repeat(heights, dims[axis_at] // parts).reshape([-1 if axis == axis_at else 1 for axis in range(len(dims))])
    return loudness


def scatter_about(own_key, extent, scale, limit, cuts=(), kind=jnp.bfloat16):
    loudness = steps_of(own_key, extent, cuts, -0.22, 0.18) if cuts else 1.0
    array = jax.random.normal(own_key, extent, jnp.float32) * scale * loudness
    return jnp.minimum(jnp.maximum(array, -limit), limit).astype(kind)


def setup_inputs(seed: int = 0) -> dict:
    key_of = jax.random.split(jax.random.key(seed), 12)
    return {
        "hidden_in": scatter_about(key_of[0], (LATENTS, SEQ, D), 1.0, 6.0, ((0, 8), (1, 2))),
        "cotangent": scatter_about(key_of[1], (LATENTS, SEQ, D), 1.0, 6.0, ((0, 8), (1, 2))),
        "ada_w": scatter_about(key_of[2], (2, D, 6 * D), D ** -0.5, 0.3125, ((0, 2), (1, 8))),
        "ada_b": scatter_about(key_of[3], (2, 6 * D), 0.25, 1.5, ((0, 2), (1, 8))),
        "qkv_w": scatter_about(key_of[4], (2, D, 3 * D), D ** -0.5, 0.3125, ((0, 2), (1, 8))),
        "proj_w": scatter_about(key_of[5], (2, D, D), (D // 4) ** -0.5, 0.625, ((0, 2), (1, 8))),
        "mlp_in_w": scatter_about(key_of[6], (2, D, FF), D ** -0.5, 0.3125, ((0, 2), (1, 8))),
        "mlp_out_w": scatter_about(key_of[7], (2, FF, D), FF ** -0.5, 0.15625, ((0, 2), (1, 8))),
        "class_table": scatter_about(key_of[8], (NCLASS, D), 1.0, 6.0, ((1, 8),)),
        "timesteps": touch_ends(jax.random.randint(key_of[9], (LATENTS,), 0, NSTEPS), jax.random.fold_in(key_of[9], 1), 0, NSTEPS - 1).astype(jnp.int32),
        "labels": touch_ends(jax.random.randint(key_of[10], (LATENTS,), 0, NCLASS), jax.random.fold_in(key_of[10], 1), 0, NCLASS - 1).astype(jnp.int32),
    }


@jax.custom_vjp
def low(v):
    return lax.optimization_barrier(v.astype(jnp.bfloat16)).astype(jnp.float32)

@jax.custom_vjp
def low_back(v):
    return v

def low_keep(v):
    return (low(v), None)

def low_pass(kept, grad):
    return (grad,)

def back_keep(v):
    return (v, None)

def back_low(kept, grad):
    return (low(grad),)
low.defvjp(low_keep, low_pass)
low_back.defvjp(back_keep, back_low)
eps_norm = 1e-06
highest = lax.Precision.HIGHEST

def sinusoid(step_ids, model_width):
    half_width = model_width // 2
    frequency = jnp.exp(-math.log(10000.0) * jnp.arange(half_width, dtype=jnp.float32) / half_width)
    angles = step_ids.astype(jnp.float32)[:, None] * frequency[None, :]
    return jnp.concatenate([jnp.cos(angles), jnp.sin(angles)], axis=1)

def normalize(values):
    center = values - lax.optimization_barrier(jnp.mean(values, axis=-1, keepdims=True))
    spread = lax.optimization_barrier(jnp.mean(center * center, axis=-1, keepdims=True))
    return center * lax.rsqrt(spread + eps_norm)

def attend(block_in):
    queries, keys_in, values_in = block_in
    scores = jnp.einsum('gqhe,gkhe->ghqk', queries, keys_in, precision=highest) * HDIM ** (-0.5)
    scores = low_back(scores)
    probability = low(jax.nn.softmax(scores, axis=-1))
    return jnp.einsum('ghqk,gkhe->gqhe', probability, values_in, precision=highest)

def apply_layer(stream, silu_low, ada_w, ada_b, qkv_w, proj_w, mlp_in_w, mlp_out_w):
    lat_count = stream.shape[0]
    modulation = jnp.dot(silu_low, ada_w, precision=highest) + ada_b
    pieces = [modulation[:, None, part_no * D:(part_no + 1) * D] for part_no in range(6)]
    first_in = low(normalize(stream) * (1.0 + pieces[1]) + pieces[0])
    qkv_all = low(low_back(jnp.einsum('bsd,de->bse', first_in, qkv_w, precision=highest)))
    group_size = math.gcd(lat_count, max(1, 4096 // SEQ))

    def heads_of(part_no):
        return qkv_all[..., part_no * D:(part_no + 1) * D].reshape(lat_count // group_size, group_size, SEQ, HEADS, HDIM)
    mixed_heads = lax.map(jax.checkpoint(attend), (heads_of(0), heads_of(1), heads_of(2)))
    mixed_heads = low(low_back(mixed_heads.reshape(lat_count, SEQ, D)))
    attn_out = low_back(jnp.einsum('bsd,de->bse', mixed_heads, proj_w, precision=highest))
    middle = stream + pieces[2] * attn_out
    second_in = low(normalize(middle) * (1.0 + pieces[4]) + pieces[3])
    hidden = low_back(jnp.einsum('bsd,df->bsf', second_in, mlp_in_w, precision=highest))
    activated = low(jax.nn.gelu(hidden, approximate=True))
    mlp_out = low_back(jnp.einsum('bsf,fd->bsd', activated, mlp_out_w, precision=highest))
    return middle + pieces[5] * mlp_out

def reference(hidden_in, cotangent, ada_w, ada_b, qkv_w, proj_w, mlp_in_w, mlp_out_w, class_table, timesteps, labels):
    floats = [member.astype(jnp.float32) for member in (hidden_in, ada_w, ada_b, qkv_w, proj_w, mlp_in_w, mlp_out_w, class_table)]

    def forward(stream, ada_all, bias_all, qkv_all, proj_all, mlp_in_all, mlp_out_all, class_rows, offset):
        condition = sinusoid(timesteps, D) + class_rows[labels]
        silu_low = low(jax.nn.silu(condition))
        first_out = apply_layer(stream, silu_low, ada_all[0], bias_all[0], qkv_all[0], proj_all[0], mlp_in_all[0], mlp_out_all[0])
        passed = low(low_back(first_out)) + offset
        second_out = apply_layer(passed, silu_low, ada_all[1], bias_all[1], qkv_all[1], proj_all[1], mlp_in_all[1], mlp_out_all[1])
        return (second_out, passed)
    offset = jnp.zeros(hidden_in.shape, jnp.float32)
    second_out, backward_fn, passed = jax.vjp(forward, *floats, offset, has_aux=True)
    gradients = backward_fn(cotangent.astype(jnp.float32))
    hidden_states = jnp.stack([passed, second_out]).astype(jnp.bfloat16)
    input_grads = jnp.stack([gradients[0], gradients[8]]).astype(jnp.bfloat16)
    return (hidden_states, input_grads, gradients[1], gradients[2], gradients[3], gradients[4], gradients[5], gradients[6], gradients[7])
```

```python
import functools
import math

import jax
import jax.numpy as jnp
from jax import lax
from jax.experimental import pallas as pl
from jax.experimental.pallas import tpu as pltpu
from jax.sharding import PartitionSpec as P

HDIM = 64
PAIR = 2 * HDIM
TILE = 256
EPS = 1e-06
SCALE = HDIM ** (-0.5)
GC = math.sqrt(2.0 / math.pi)
GA = 0.044715
F32 = jnp.float32
BF16 = jnp.bfloat16
NT = (((1,), (1,)), ((), ()))
TN = (((0,), (0,)), ((), ()))
HIGH = lax.Precision.HIGHEST


def mm(a, b, dims=(((1,), (0,)), ((), ()))):
    return lax.dot_general(a, b, dims, preferred_element_type=F32)


def norm_of(v):
    center = v - jnp.mean(v, axis=-1, keepdims=True)
    rs = lax.rsqrt(jnp.mean(center * center, axis=-1, keepdims=True) + EPS)
    return center * rs, rs


def norm_back(n, rs, u):
    return rs * (
        u - jnp.mean(u, axis=-1, keepdims=True) - n * jnp.mean(u * n, axis=-1, keepdims=True)
    )


def row_loop(count, body):
    def step(i, carry):
        body(pl.ds(pl.multiple_of(i * TILE, TILE), TILE))
        return carry

    lax.fori_loop(0, count // TILE, step, 0)


def head_masks(rows):
    lane = lax.broadcasted_iota(jnp.int32, (rows, PAIR), 1)
    return [lane < HDIM, lane >= HDIM]


def fwd_kernel(x_ref, mod_ref, wqkv, wproj, wmi, wmo, y_ref, qkv_ref, lse_ref, mix_ref, mid_ref, ao_ref, mo_ref, vt_ref):
    tok, d = x_ref.shape
    mod = mod_ref[...]
    sh1, sc1, g1, sh2, sc2, g2 = [mod[i : i + 1] for i in range(6)]

    def project(rows):
        n, _ = norm_of(x_ref[rows, :].astype(F32))
        first = (n * (1.0 + sc1) + sh1).astype(BF16)
        qkv = mm(first, wqkv[...])
        qkv_ref[rows, :] = qkv.astype(BF16)
        vt_ref[:, rows] = qkv[:, 2 * d :].T.astype(BF16)

    row_loop(tok, project)
    lse_ref[...] = jnp.zeros_like(lse_ref)
    masks = head_masks(TILE)
    for p in range(d // PAIR):
        lo = p * PAIR

        def attend(rows, p=p, lo=lo):
            q = qkv_ref[rows, lo : lo + PAIR] * SCALE
            k = qkv_ref[:, d + lo : d + lo + PAIR]
            outs = []
            for h in range(2):
                qm = jnp.where(masks[h], q, jnp.zeros_like(q))
                st = mm(k, qm, NT)
                top = jnp.max(st, axis=0, keepdims=True)
                e = jnp.exp(st - top)
                total = jnp.sum(e, axis=0, keepdims=True)
                row = 2 * p + h
                lse_ref[row : row + 1, rows] = top + jnp.log(total)
                ot = mm(vt_ref[lo + h * HDIM : lo + (h + 1) * HDIM, :], e.astype(BF16))
                outs.append(ot / total)
            mix_ref[rows, lo : lo + PAIR] = jnp.concatenate(outs, axis=0).T.astype(BF16)

        row_loop(tok, attend)

    def feed(rows):
        ao = mm(mix_ref[rows, :], wproj[...])
        mid = x_ref[rows, :].astype(F32) + g1 * ao
        ao_ref[rows, :] = ao.astype(BF16)
        mid_ref[rows, :] = mid
        n, _ = norm_of(mid)
        second = (n * (1.0 + sc2) + sh2).astype(BF16)
        hid = mm(second, wmi[...])
        act = 0.5 * hid * (1.0 + jnp.tanh(GC * (hid + GA * hid * hid * hid)))
        mo = mm(act.astype(BF16), wmo[...])
        mo_ref[rows, :] = mo.astype(BF16)
        y_ref[rows, :] = (mid + g2 * mo).astype(BF16)

    row_loop(tok, feed)


def bwd_kernel(g_ref, x_ref, mod_ref, wqkv, wproj, wmi, wmo, qkv_ref, lse_ref, mix_ref, mid_ref, ao_ref, mo_ref,
               gin_ref, gmod_ref, dqkvw_ref, dproj_ref, dmi_ref, dmo_ref,
               aqkv, aproj, ami, amo, kt_ref, gmid_ref, gmx_ref, delta_ref, dqkv_ref, dk_acc, dv_acc):
    tok, d = x_ref.shape
    heads = d // HDIM
    mod = mod_ref[...]
    sh1, sc1, g1, sh2, sc2, g2 = [mod[i : i + 1] for i in range(6)]
    for acc in (gmod_ref, aqkv, aproj, ami, amo):
        acc[...] = jnp.zeros_like(acc)
    sel = (
        lax.broadcasted_iota(jnp.int32, (8, d), 1) // HDIM == lax.broadcasted_iota(jnp.int32, (8, d), 0)
    ).astype(F32)

    def add_mod(i, value):
        gmod_ref[i : i + 1, :] += jnp.sum(value, axis=0, keepdims=True)

    def feed_back(rows):
        kt_ref[:, rows] = qkv_ref[rows, d : 2 * d].astype(F32).T.astype(BF16)
        n, rs = norm_of(mid_ref[rows, :])
        second = (n * (1.0 + sc2) + sh2).astype(BF16)
        hid = mm(second, wmi[...])
        sq = hid * hid
        th = jnp.tanh(GC * (hid + GA * hid * sq))
        half = 0.5 * (1.0 + th)
        act = (hid * half).astype(BF16)
        slope = half + 0.5 * hid * (1.0 - th * th) * (GC * (1.0 + 3.0 * GA * sq))
        g = g_ref[rows, :].astype(F32)
        gm = (g2 * g).astype(BF16)
        amo[...] += mm(act, gm, TN)
        gh = (mm(gm, wmo[...], NT) * slope).astype(BF16)
        ami[...] += mm(second, gh, TN)
        gs = mm(gh, wmi[...], NT)
        add_mod(3, gs)
        add_mod(4, gs * n)
        add_mod(5, g * mo_ref[rows, :].astype(F32))
        gmid = g + norm_back(n, rs, gs * (1.0 + sc2))
        gmid_ref[rows, :] = gmid
        add_mod(2, gmid * ao_ref[rows, :].astype(F32))
        ga = (g1 * gmid).astype(BF16)
        mix = mix_ref[rows, :]
        aproj[...] += mm(mix, ga, TN)
        gmx = mm(ga, wproj[...], NT).astype(BF16)
        gmx_ref[rows, :] = gmx
        delta_ref[:, rows] = lax.dot_general(
            sel, gmx.astype(F32) * mix.astype(F32), NT, precision=HIGH, preferred_element_type=F32
        )

    row_loop(tok, feed_back)
    masks = head_masks(TILE)
    for p in range(d // PAIR):
        lo = p * PAIR
        dk_acc[...] = jnp.zeros_like(dk_acc)
        dv_acc[...] = jnp.zeros_like(dv_acc)

        def attend_back(rows, p=p, lo=lo):
            q = qkv_ref[rows, lo : lo + PAIR] * SCALE
            do = gmx_ref[rows, lo : lo + PAIR]
            k = qkv_ref[:, d + lo : d + lo + PAIR]
            v = qkv_ref[:, 2 * d + lo : 2 * d + lo + PAIR]
            outs = []
            for h in range(2):
                row = 2 * p + h
                qm = jnp.where(masks[h], q, jnp.zeros_like(q))
                dom = jnp.where(masks[h], do, jnp.zeros_like(do))
                pt = jnp.exp(mm(k, qm, NT) - lse_ref[row : row + 1, rows])
                dv_acc[...] += mm(pt.astype(BF16), dom)
                ds = (pt * (mm(v, dom, NT) - delta_ref[row : row + 1, rows])).astype(BF16)
                dk_acc[...] += mm(ds, qm)
                outs.append(mm(kt_ref[lo + h * HDIM : lo + (h + 1) * HDIM, :], ds))
            dqkv_ref[rows, lo : lo + PAIR] = (jnp.concatenate(outs, axis=0) * SCALE).T.astype(BF16)

        row_loop(tok, attend_back)
        dqkv_ref[:, d + lo : d + lo + PAIR] = dk_acc[...].astype(BF16)
        dqkv_ref[:, 2 * d + lo : 2 * d + lo + PAIR] = dv_acc[...].astype(BF16)

    def project_back(rows):
        n, rs = norm_of(x_ref[rows, :].astype(F32))
        first = (n * (1.0 + sc1) + sh1).astype(BF16)
        dqkv = dqkv_ref[rows, :]
        aqkv[...] += mm(first, dqkv, TN)
        gf = mm(dqkv, wqkv[...], NT)
        add_mod(0, gf)
        add_mod(1, gf * n)
        gin_ref[rows, :] = (gmid_ref[rows, :] + norm_back(n, rs, gf * (1.0 + sc1))).astype(BF16)

    row_loop(tok, project_back)
    dqkvw_ref[...] = aqkv[...].astype(BF16)
    dproj_ref[...] = aproj[...].astype(BF16)
    dmi_ref[...] = ami[...].astype(BF16)
    dmo_ref[...] = amo[...].astype(BF16)


def vmem(count):
    return [pl.BlockSpec(memory_space=pltpu.VMEM)] * count


def run_forward(x, mod, weights):
    tok, d = x.shape
    sds = jax.ShapeDtypeStruct
    ff = weights[2].shape[1]
    return pl.pallas_call(
        fwd_kernel,
        out_shape=[
            sds((tok, d), BF16),
            sds((tok, 3 * d), BF16),
            sds((8, tok), F32),
            sds((tok, d), BF16),
            sds((tok, d), F32),
            sds((tok, d), BF16),
            sds((tok, d), BF16),
        ],
        in_specs=vmem(6),
        out_specs=vmem(7),
        scratch_shapes=[pltpu.VMEM((d, tok), BF16)],
        compiler_params=pltpu.CompilerParams(vmem_limit_bytes=48 * 2**20),
        cost_estimate=pl.CostEstimate(
            flops=2 * tok * d * (4 * d + 2 * ff + 8 * tok), bytes_accessed=16 * 2**20, transcendentals=0
        ),
    )(x, mod, *weights)


def run_backward(g, x, mod, weights, saved):
    tok, d = x.shape
    sds = jax.ShapeDtypeStruct
    ff = weights[2].shape[1]
    shapes = [(d, 3 * d), (d, d), (d, ff), (ff, d)]
    return pl.pallas_call(
        bwd_kernel,
        out_shape=[sds((tok, d), BF16), sds((8, d), F32)] + [sds(s, BF16) for s in shapes],
        in_specs=vmem(13),
        out_specs=vmem(6),
        scratch_shapes=[pltpu.VMEM(s, F32) for s in shapes]
        + [
            pltpu.VMEM((d, tok), BF16),
            pltpu.VMEM((tok, d), F32),
            pltpu.VMEM((tok, d), BF16),
            pltpu.VMEM((8, tok), F32),
            pltpu.VMEM((tok, 3 * d), BF16),
            pltpu.VMEM((tok, PAIR), F32),
            pltpu.VMEM((tok, PAIR), F32),
        ],
        compiler_params=pltpu.CompilerParams(vmem_limit_bytes=56 * 2**20),
        cost_estimate=pl.CostEstimate(
            flops=4 * tok * d * (4 * d + 3 * ff + 10 * tok), bytes_accessed=24 * 2**20, transcendentals=0
        ),
    )(g, x, mod, *weights, *saved)


def sinusoid(step_ids, model_width):
    half_width = model_width // 2
    frequency = jnp.exp(-math.log(10000.0) * jnp.arange(half_width, dtype=F32) / half_width)
    angles = step_ids.astype(F32)[:, None] * frequency[None, :]
    return jnp.concatenate([jnp.cos(angles), jnp.sin(angles)], axis=1)


def swap_axis(value, axis):
    return lax.ppermute(value, axis, [(0, 1), (1, 0)])


def take_latent(block, section, context):
    pair = lax.dynamic_slice_in_dim(block, 2 * section, 2, 0)
    own = lax.dynamic_index_in_dim(pair, context, 0, keepdims=False)
    other = swap_axis(lax.dynamic_index_in_dim(pair, 1 - context, 0, keepdims=False), "context")
    first = context == 0
    return jnp.concatenate([jnp.where(first, own, other), jnp.where(first, other, own)], axis=0)


def spread_out(zero, one):
    tok, d = zero.shape
    both = jnp.concatenate([zero, one], axis=0).reshape(4, tok // 2, d)
    return lax.all_to_all(both, ("section", "context"), 0, 0, tiled=True)[None]


def per_device(hidden_in, cotangent, ada_w, ada_b, qkv_w, proj_w, mlp_in_w, mlp_out_w, class_table, timesteps, labels):
    section = lax.axis_index("section")
    dp = lax.axis_index("dp")
    context = lax.axis_index("context")
    d = hidden_in.shape[-1]
    cols = class_table.shape[1]

    steps_all = lax.all_gather(timesteps, "dp", tiled=True)
    labels_all = lax.all_gather(labels, "dp", tiled=True)

    def gather(w):
        w = w[0]
        half = w.shape[0] // 2
        mine = lax.dynamic_slice_in_dim(w, context * half, half, 0)
        full = lax.all_gather(mine, ("section", "dp", "context"), axis=0, tiled=True)
        rows = full.shape[0] // 2
        return full[:rows], full[rows:]

    pairs = [gather(w) for w in (qkv_w, proj_w, mlp_in_w, mlp_out_w)]
    weights = [tuple(pair[layer] for pair in pairs) for layer in range(2)]
    hidden = take_latent(hidden_in, section, context)
    cot = take_latent(cotangent, section, context)

    one_hot = (labels_all[:, None] == jnp.arange(class_table.shape[0], dtype=jnp.int32)[None, :]).astype(F32)
    phase = lax.dynamic_slice_in_dim(sinusoid(steps_all, d), dp * cols, cols, 1)
    condition = phase + jnp.dot(one_hot.astype(BF16), class_table, preferred_element_type=F32)
    silu_low = jax.nn.silu(condition).astype(BF16)
    partial = jnp.dot(silu_low, ada_w[0], preferred_element_type=F32)
    wide = ada_b.shape[1]
    bias = lax.dynamic_update_slice_in_dim(
        jnp.zeros((1, partial.shape[1]), F32), ada_b.astype(F32), dp * wide, 1
    )
    mods = lax.psum_scatter(partial + bias, "dp", scatter_dimension=0, tiled=True)
    mods = lax.all_gather(mods, "section")
    mods = lax.dynamic_index_in_dim(mods, 2 * section + context, 1, keepdims=False)
    mods = jnp.pad(mods.reshape(2, 6, d), ((0, 0), (0, 2), (0, 0)))

    passed, *saved0 = run_forward(hidden, mods[0], weights[0])
    second, *saved1 = run_forward(passed, mods[1], weights[1])
    states = spread_out(passed, second)

    def reduce(grads):
        return [lax.psum_scatter(g, ("dp", "context"), scatter_dimension=0, tiled=True) for g in grads]

    g0, gmod1, *wg1 = run_backward(cot, passed, mods[1], weights[1], saved1)
    parts1 = reduce(wg1)
    gin, gmod0, *wg0 = run_backward(g0, hidden, mods[0], weights[0], saved0)
    parts0 = reduce(wg0)
    grads = spread_out(gin, g0)

    upper = section == 1
    shares = []
    for p0, p1 in zip(parts0, parts1):
        other = swap_axis(jnp.where(upper, p0, p1), "section")
        mine = jnp.where(upper, p1, p0).astype(F32) + other.astype(F32)
        shares.append(lax.all_gather(mine, "context", axis=0, tiled=True)[None])

    def all_latents(gmod):
        return lax.all_gather(gmod[:6].reshape(-1), ("dp", "section", "context"))

    gm = jnp.where(upper, all_latents(gmod1), all_latents(gmod0))
    grad_ada = jnp.einsum("ld,le->de", silu_low.astype(F32), gm, precision=HIGH)[None]
    grad_bias = lax.dynamic_slice_in_dim(jnp.sum(gm, axis=0, keepdims=True), dp * wide, wide, 1)
    grad_silu = jnp.einsum("le,de->ld", gm, ada_w[0].astype(F32), precision=HIGH)
    grad_silu = lax.psum(grad_silu, "section")
    grad_cond = jax.vjp(jax.nn.silu, condition)[1](grad_silu)[0]
    table = jnp.einsum("lc,ld->cd", one_hot, grad_cond, precision=HIGH)
    return (states, grads, grad_ada, grad_bias, *shares, table)


def solution(mesh):
    wide = P("section", "dp", None)
    tokens = P("dp", "context", None)
    in_specs = (tokens, tokens, wide, P("section", "dp"), wide, wide, wide, wide, P(None, "dp"), P("dp"), P("dp"))
    stacked = P("section", "dp", "context", None)
    out_specs = (stacked, stacked, wide, P("section", "dp"), wide, wide, wide, wide, P(None, "dp"))
    return jax.shard_map(per_device, mesh=mesh, in_specs=in_specs, out_specs=out_specs, check_vma=False)
```

```python
import functools
import math

import jax
import jax.numpy as jnp
from jax import lax
from jax.experimental import pallas as pl
from jax.experimental.pallas import tpu as pltpu
from jax.sharding import PartitionSpec as P

HDIM = 64
PAIR = 2 * HDIM
TILE = 256
EPS = 1e-06
SCALE = HDIM ** (-0.5)
GC = math.sqrt(2.0 / math.pi)
GA = 0.044715
F32 = jnp.float32
BF16 = jnp.bfloat16
NT = (((1,), (1,)), ((), ()))
TN = (((0,), (0,)), ((), ()))
HIGH = lax.Precision.HIGHEST


def mm(a, b, dims=(((1,), (0,)), ((), ()))):
    return lax.dot_general(a, b, dims, preferred_element_type=F32)


def norm_of(v):
    center = v - jnp.mean(v, axis=-1, keepdims=True)
    rs = lax.rsqrt(jnp.mean(center * center, axis=-1, keepdims=True) + EPS)
    return center * rs, rs


def norm_back(n, rs, u):
    return rs * (
        u - jnp.mean(u, axis=-1, keepdims=True) - n * jnp.mean(u * n, axis=-1, keepdims=True)
    )


def row_loop(count, body):
    def step(i, carry):
        body(pl.ds(pl.multiple_of(i * TILE, TILE), TILE))
        return carry

    lax.fori_loop(0, count // TILE, step, 0)


def head_masks(rows):
    lane = lax.broadcasted_iota(jnp.int32, (rows, PAIR), 1)
    return [lane < HDIM, lane >= HDIM]


def fwd_kernel(x_ref, mod_ref, wqkv, wproj, wmi, wmo, y_ref, qkv_ref, lse_ref, mix_ref, mid_ref, ao_ref, mo_ref, vt_ref):
    tok, d = x_ref.shape
    mod = mod_ref[...]
    sh1, sc1, g1, sh2, sc2, g2 = [mod[i : i + 1] for i in range(6)]

    def project(rows):
        n, _ = norm_of(x_ref[rows, :].astype(F32))
        first = (n * (1.0 + sc1) + sh1).astype(BF16)
        qkv = mm(first, wqkv[...])
        qkv_ref[rows, :] = qkv.astype(BF16)
        vt_ref[:, rows] = qkv[:, 2 * d :].T.astype(BF16)

    row_loop(tok, project)
    lse_ref[...] = jnp.zeros_like(lse_ref)
    masks = head_masks(TILE)
    for p in range(d // PAIR):
        lo = p * PAIR

        def attend(rows, p=p, lo=lo):
            q = qkv_ref[rows, lo : lo + PAIR] * SCALE
            k = qkv_ref[:, d + lo : d + lo + PAIR]
            outs = []
            for h in range(2):
                qm = jnp.where(masks[h], q, jnp.zeros_like(q))
                st = mm(k, qm, NT)
                top = jnp.max(st, axis=0, keepdims=True)
                e = jnp.exp(st - top)
                total = jnp.sum(e, axis=0, keepdims=True)
                row = 2 * p + h
                lse_ref[row : row + 1, rows] = top + jnp.log(total)
                ot = mm(vt_ref[lo + h * HDIM : lo + (h + 1) * HDIM, :], e.astype(BF16))
                outs.append(ot / total)
            mix_ref[rows, lo : lo + PAIR] = jnp.concatenate(outs, axis=0).T.astype(BF16)

        row_loop(tok, attend)

    def feed(rows):
        ao = mm(mix_ref[rows, :], wproj[...])
        mid = x_ref[rows, :].astype(F32) + g1 * ao
        ao_ref[rows, :] = ao.astype(BF16)
        mid_ref[rows, :] = mid
        n, _ = norm_of(mid)
        second = (n * (1.0 + sc2) + sh2).astype(BF16)
        hid = mm(second, wmi[...])
        act = 0.5 * hid * (1.0 + jnp.tanh(GC * (hid + GA * hid * hid * hid)))
        mo = mm(act.astype(BF16), wmo[...])
        mo_ref[rows, :] = mo.astype(BF16)
        y_ref[rows, :] = (mid + g2 * mo).astype(BF16)

    row_loop(tok, feed)


def bwd_kernel(g_ref, x_ref, mod_ref, wqkv, wproj, wmi, wmo, qkv_ref, lse_ref, mix_ref, mid_ref, ao_ref, mo_ref,
               gin_ref, gmod_ref, aqkv, aproj, ami, amo,
               kt_ref, gmid_ref, gmx_ref, delta_ref, dqkv_ref, dk_acc, dv_acc):
    tok, d = x_ref.shape
    heads = d // HDIM
    mod = mod_ref[...]
    sh1, sc1, g1, sh2, sc2, g2 = [mod[i : i + 1] for i in range(6)]
    for acc in (gmod_ref, aqkv, aproj, ami, amo):
        acc[...] = jnp.zeros_like(acc)
    sel = (
        lax.broadcasted_iota(jnp.int32, (8, d), 1) // HDIM == lax.broadcasted_iota(jnp.int32, (8, d), 0)
    ).astype(F32)

    def add_mod(i, value):
        gmod_ref[i : i + 1, :] += jnp.sum(value, axis=0, keepdims=True)

    def feed_back(rows):
        kt_ref[:, rows] = qkv_ref[rows, d : 2 * d].astype(F32).T.astype(BF16)
        n, rs = norm_of(mid_ref[rows, :])
        second = (n * (1.0 + sc2) + sh2).astype(BF16)
        hid = mm(second, wmi[...])
        sq = hid * hid
        th = jnp.tanh(GC * (hid + GA * hid * sq))
        half = 0.5 * (1.0 + th)
        act = (hid * half).astype(BF16)
        slope = half + 0.5 * hid * (1.0 - th * th) * (GC * (1.0 + 3.0 * GA * sq))
        g = g_ref[rows, :].astype(F32)
        gm = (g2 * g).astype(BF16)
        amo[...] += mm(act, gm, TN)
        gh = (mm(gm, wmo[...], NT) * slope).astype(BF16)
        ami[...] += mm(second, gh, TN)
        gs = mm(gh, wmi[...], NT)
        add_mod(3, gs)
        add_mod(4, gs * n)
        add_mod(5, g * mo_ref[rows, :].astype(F32))
        gmid = g + norm_back(n, rs, gs * (1.0 + sc2))
        gmid_ref[rows, :] = gmid
        add_mod(2, gmid * ao_ref[rows, :].astype(F32))
        ga = (g1 * gmid).astype(BF16)
        mix = mix_ref[rows, :]
        aproj[...] += mm(mix, ga, TN)
        gmx = mm(ga, wproj[...], NT).astype(BF16)
        gmx_ref[rows, :] = gmx
        delta_ref[:, rows] = lax.dot_general(
            sel, gmx.astype(F32) * mix.astype(F32), NT, precision=HIGH, preferred_element_type=F32
        )

    row_loop(tok, feed_back)
    masks = head_masks(TILE)
    for p in range(d // PAIR):
        lo = p * PAIR
        dk_acc[...] = jnp.zeros_like(dk_acc)
        dv_acc[...] = jnp.zeros_like(dv_acc)

        def attend_back(rows, p=p, lo=lo):
            q = qkv_ref[rows, lo : lo + PAIR] * SCALE
            do = gmx_ref[rows, lo : lo + PAIR]
            k = qkv_ref[:, d + lo : d + lo + PAIR]
            v = qkv_ref[:, 2 * d + lo : 2 * d + lo + PAIR]
            outs = []
            for h in range(2):
                row = 2 * p + h
                qm = jnp.where(masks[h], q, jnp.zeros_like(q))
                dom = jnp.where(masks[h], do, jnp.zeros_like(do))
                pt = jnp.exp(mm(k, qm, NT) - lse_ref[row : row + 1, rows])
                dv_acc[...] += mm(pt.astype(BF16), dom)
                ds = (pt * (mm(v, dom, NT) - delta_ref[row : row + 1, rows])).astype(BF16)
                dk_acc[...] += mm(ds, qm)
                outs.append(mm(kt_ref[lo + h * HDIM : lo + (h + 1) * HDIM, :], ds))
            dqkv_ref[rows, lo : lo + PAIR] = (jnp.concatenate(outs, axis=0) * SCALE).T.astype(BF16)

        row_loop(tok, attend_back)
        dqkv_ref[:, d + lo : d + lo + PAIR] = dk_acc[...].astype(BF16)
        dqkv_ref[:, 2 * d + lo : 2 * d + lo + PAIR] = dv_acc[...].astype(BF16)

    def project_back(rows):
        n, rs = norm_of(x_ref[rows, :].astype(F32))
        first = (n * (1.0 + sc1) + sh1).astype(BF16)
        dqkv = dqkv_ref[rows, :]
        aqkv[...] += mm(first, dqkv, TN)
        gf = mm(dqkv, wqkv[...], NT)
        add_mod(0, gf)
        add_mod(1, gf * n)
        gin_ref[rows, :] = (gmid_ref[rows, :] + norm_back(n, rs, gf * (1.0 + sc1))).astype(BF16)

    row_loop(tok, project_back)


def vmem(count):
    return [pl.BlockSpec(memory_space=pltpu.VMEM)] * count


def run_forward(x, mod, weights):
    tok, d = x.shape
    sds = jax.ShapeDtypeStruct
    ff = weights[2].shape[1]
    return pl.pallas_call(
        fwd_kernel,
        out_shape=[
            sds((tok, d), BF16),
            sds((tok, 3 * d), BF16),
            sds((8, tok), F32),
            sds((tok, d), BF16),
            sds((tok, d), F32),
            sds((tok, d), BF16),
            sds((tok, d), BF16),
        ],
        in_specs=vmem(6),
        out_specs=vmem(7),
        scratch_shapes=[pltpu.VMEM((d, tok), BF16)],
        compiler_params=pltpu.CompilerParams(vmem_limit_bytes=48 * 2**20),
        cost_estimate=pl.CostEstimate(
            flops=2 * tok * d * (4 * d + 2 * ff + 8 * tok), bytes_accessed=16 * 2**20, transcendentals=0
        ),
    )(x, mod, *weights)


def run_backward(g, x, mod, weights, saved):
    tok, d = x.shape
    sds = jax.ShapeDtypeStruct
    ff = weights[2].shape[1]
    shapes = [(d, 3 * d), (d, d), (d, ff), (ff, d)]
    return pl.pallas_call(
        bwd_kernel,
        out_shape=[sds((tok, d), BF16), sds((8, d), F32)] + [sds(s, F32) for s in shapes],
        in_specs=vmem(13),
        out_specs=vmem(6),
        scratch_shapes=[
            pltpu.VMEM((d, tok), BF16),
            pltpu.VMEM((tok, d), F32),
            pltpu.VMEM((tok, d), BF16),
            pltpu.VMEM((8, tok), F32),
            pltpu.VMEM((tok, 3 * d), BF16),
            pltpu.VMEM((tok, PAIR), F32),
            pltpu.VMEM((tok, PAIR), F32),
        ],
        compiler_params=pltpu.CompilerParams(vmem_limit_bytes=56 * 2**20),
        cost_estimate=pl.CostEstimate(
            flops=4 * tok * d * (4 * d + 3 * ff + 10 * tok), bytes_accessed=24 * 2**20, transcendentals=0
        ),
    )(g, x, mod, *weights, *saved)


def sinusoid(step_ids, model_width):
    half_width = model_width // 2
    frequency = jnp.exp(-math.log(10000.0) * jnp.arange(half_width, dtype=F32) / half_width)
    angles = step_ids.astype(F32)[:, None] * frequency[None, :]
    return jnp.concatenate([jnp.cos(angles), jnp.sin(angles)], axis=1)


def swap_axis(value, axis):
    return lax.ppermute(value, axis, [(0, 1), (1, 0)])


def take_latent(block, section, context):
    pair = lax.dynamic_slice_in_dim(block, 2 * section, 2, 0)
    own = lax.dynamic_index_in_dim(pair, context, 0, keepdims=False)
    other = swap_axis(lax.dynamic_index_in_dim(pair, 1 - context, 0, keepdims=False), "context")
    first = context == 0
    return jnp.concatenate([jnp.where(first, own, other), jnp.where(first, other, own)], axis=0)


def spread_out(zero, one):
    tok, d = zero.shape
    both = jnp.concatenate([zero, one], axis=0).reshape(4, tok // 2, d)
    return lax.all_to_all(both, ("section", "context"), 0, 0, tiled=True)[None]


def per_device(hidden_in, cotangent, ada_w, ada_b, qkv_w, proj_w, mlp_in_w, mlp_out_w, class_table, timesteps, labels):
    section = lax.axis_index("section")
    dp = lax.axis_index("dp")
    context = lax.axis_index("context")
    d = hidden_in.shape[-1]
    cols = class_table.shape[1]

    steps_all = lax.all_gather(timesteps, "dp", tiled=True)
    labels_all = lax.all_gather(labels, "dp", tiled=True)

    half = qkv_w.shape[1] // 2
    packed = jnp.concatenate(
        [w[0].reshape(2 * half, -1) for w in (qkv_w, proj_w, mlp_in_w, mlp_out_w)], axis=1
    )
    packed = lax.dynamic_slice_in_dim(packed, context * half, half, 0)
    packed = lax.all_gather(packed, ("section", "dp", "context"), axis=0, tiled=True)
    packed = packed.reshape(2, d, packed.shape[1])
    ff = mlp_in_w.shape[2]

    def unpack(block):
        parts = jnp.split(block, [3 * d, 4 * d, 4 * d + ff], axis=1)
        return parts[:3] + [parts[3].reshape(-1, d)]

    weights = [unpack(packed[layer]) for layer in range(2)]
    hidden = take_latent(hidden_in, section, context)
    cot = take_latent(cotangent, section, context)

    one_hot = (labels_all[:, None] == jnp.arange(class_table.shape[0], dtype=jnp.int32)[None, :]).astype(F32)
    phase = lax.dynamic_slice_in_dim(sinusoid(steps_all, d), dp * cols, cols, 1)
    condition = phase + jnp.dot(one_hot.astype(BF16), class_table, preferred_element_type=F32)
    silu_low = jax.nn.silu(condition).astype(BF16)
    partial = jnp.dot(silu_low, ada_w[0], preferred_element_type=F32)
    wide = ada_b.shape[1]
    bias = lax.dynamic_update_slice_in_dim(
        jnp.zeros((1, partial.shape[1]), F32), ada_b.astype(F32), dp * wide, 1
    )
    mods = lax.psum_scatter(partial + bias, "dp", scatter_dimension=0, tiled=True)
    mods = lax.all_gather(mods, "section")
    mods = lax.dynamic_index_in_dim(mods, 2 * section + context, 1, keepdims=False)
    mods = jnp.pad(mods.reshape(2, 6, d), ((0, 0), (0, 2), (0, 0)))

    passed, *saved0 = run_forward(hidden, mods[0], weights[0])
    second, *saved1 = run_forward(passed, mods[1], weights[1])
    states = spread_out(passed, second)

    def reduce(grads):
        flat = jnp.concatenate([g.reshape(d, -1) for g in grads], axis=1)
        return lax.psum_scatter(flat, ("dp", "context"), scatter_dimension=0, tiled=True)

    g0, gmod1, *wg1 = run_backward(cot, passed, mods[1], weights[1], saved1)
    part1 = reduce(wg1)
    gin, gmod0, *wg0 = run_backward(g0, hidden, mods[0], weights[0], saved0)
    part0 = reduce(wg0)
    grads = spread_out(gin, g0)

    upper = section == 1
    other = swap_axis(jnp.where(upper, part0, part1).astype(BF16), "section")
    mine = jnp.where(upper, part1, part0) + other.astype(F32)
    shares = [share[None] for share in unpack(lax.all_gather(mine, "context", axis=0, tiled=True))]

    gmods = jnp.stack([gmod0[:6].reshape(-1), gmod1[:6].reshape(-1)])
    gmods = lax.all_gather(gmods, ("dp", "section", "context"))
    gm = lax.dynamic_index_in_dim(gmods, section, 1, keepdims=False)
    grad_ada = jnp.einsum("ld,le->de", silu_low.astype(F32), gm, precision=HIGH)[None]
    grad_bias = lax.dynamic_slice_in_dim(jnp.sum(gm, axis=0, keepdims=True), dp * wide, wide, 1)
    grad_silu = jnp.einsum("le,de->ld", gm, ada_w[0].astype(F32), precision=HIGH)
    grad_silu = lax.psum(grad_silu, "section")
    grad_cond = jax.vjp(jax.nn.silu, condition)[1](grad_silu)[0]
    table = jnp.einsum("lc,ld->cd", one_hot, grad_cond, precision=HIGH)
    return (states, grads, grad_ada, grad_bias, *shares, table)


def solution(mesh):
    wide = P("section", "dp", None)
    tokens = P("dp", "context", None)
    in_specs = (tokens, tokens, wide, P("section", "dp"), wide, wide, wide, wide, P(None, "dp"), P("dp"), P("dp"))
    stacked = P("section", "dp", "context", None)
    out_specs = (stacked, stacked, wide, P("section", "dp"), wide, wide, wide, wide, P(None, "dp"))
    return jax.shard_map(per_device, mesh=mesh, in_specs=in_specs, out_specs=out_specs, check_vma=False)
```
